32 devices in a mesh: groups: 2 (over x), ctx: 16 (over z, y, core).
Axes of the slice: x: 2, y: 2, z: 4, core: 2. Of those that a mesh axis runs over, the one named last changes fastest.
Arguments:
- ttt_query: bfloat16 [4096, 2048], P(('groups', 'ctx')), parts along dimension 0, may hold values from -6 to 6
- ttt_key: bfloat16 [4096, 2048], P(('groups', 'ctx')), parts along dimension 0, may hold values from -6 to 6
- ttt_value: bfloat16 [4096, 2048], P(('groups', 'ctx')), parts along dimension 0, may hold values from -6 to 6
- lr_logit: float32 [4096, 32], P(('groups', 'ctx')), parts along dimension 0, may hold values from -8 to 8
- lr_base: float32 [32], replicated, may hold values from 0.001953125 to 0.125
- init_weight: float32 [32, 64, 64], replicated, may hold values from -0.75 to 0.75
- attn_query: bfloat16 [4096, 2048], P(('groups', 'ctx')), parts along dimension 0, may hold values from -64 to 64
- attn_key: bfloat16 [4096, 2048], P(('groups', 'ctx')), parts along dimension 0, may hold values from -4 to 4
- attn_value: bfloat16 [4096, 2048], P(('groups', 'ctx')), parts along dimension 0, may hold values from -6 to 6
- gain_ttt: float32 [2048], replicated, may hold values from 0.5 to 1.5
- gain_attn: float32 [2048], replicated, may hold values from 0.5 to 1.5
Outputs:
- mixed: bfloat16 [4096, 2048], P(('groups', 'ctx')), parts along dimension 0
The draws below stay inside these ranges and needn't reach their ends.
There are 2 independent parts, one for each index of `groups`. The reference program is written for one: setup_inputs(seed, part) draws one part's arguments, and reference() takes and returns one part's arrays. A program takes and returns all parts, laid end to end along the dimension named above; an argument that names none is the same for every part. Nothing has to cross between parts.
All inputs are finite; a program needn't handle non-finite values.
Results may differ from the reference program's by a relative error of at most 0.0036.
Values may be sent and summed in bfloat16 or wider, within the bound.
A program may use at most 320 MiB of HBM per device.

```python
import math
import jax
import jax.numpy as jnp
from jax import lax

D = 2048
HEADS = 32
HD = 64
MB = 16
WIN_BLOCKS = 2
L_DEV = 128
TOKENS = 2048
N_CTX = 16


def pair_draw(key):
    base = jax.random.fold_in(key, 4242)
    first, second = jax.random.split(base, 2)
    keys = jnp.clip(jax.random.normal(first, (TOKENS, D), jnp.float32), -4.0, 4.0)
    query = jnp.clip(jax.random.normal(second, (TOKENS, D), jnp.float32), -4.0, 4.0)
    return (query, keys)


def draw_attn_query(key, part):
    return pair_draw(key)[0].astype(jnp.bfloat16)


def draw_attn_key(key, part):
    return pair_draw(key)[1].astype(jnp.bfloat16)


def levels(key, shape, cuts, low, high):
    factor_of = 1.0
    for axis_at, blocks in cuts:
        draws = jax.random.uniform(jax.random.fold_in(jax.random.fold_in(key, 6), axis_at), (blocks,), jnp.float32, low / len(cuts), high / len(cuts))
        factor_of = factor_of * jnp.repeat(jnp.exp(draws), shape[axis_at] // blocks).reshape((-1,) + (1,) * (len(shape) - 1 - axis_at))
    return factor_of


def scatter_about(own_key, shape, scale, reach, cuts=(), kind=jnp.bfloat16):
    factor_of = levels(own_key, shape, cuts, -0.22, 0.18) if cuts else 1.0
    entries = jax.random.normal(own_key, shape, jnp.float32) * scale * factor_of
    return jnp.minimum(jnp.maximum(entries, -reach), reach).astype(kind)


def setup_inputs(seed: int = 0, part: int = 0) -> dict:
    splits = jax.random.split(jax.random.key(seed), 12)
    own_keys = jax.random.split(jax.random.fold_in(splits[11], part), 12)
    return {
        "ttt_query": scatter_about(own_keys[0], (TOKENS, D), 1.0, 6.0, ((0, 16),)),
        "ttt_key": scatter_about(own_keys[1], (TOKENS, D), 1.0, 6.0, ((0, 16),)),
        "ttt_value": scatter_about(own_keys[2], (TOKENS, D), 1.0, 6.0, ((0, 16),)),
        "lr_logit": scatter_about(own_keys[3], (TOKENS, HEADS), 2.5, 8.0, ((0, 16),), jnp.float32),
        "lr_base": jnp.clip(jnp.exp(jax.random.uniform(splits[4], (HEADS,), jnp.float32, math.log(0.001953125), math.log(0.125))), 0.001953125, 0.125),
        "init_weight": scatter_about(splits[5], (HEADS, HD, HD), HD ** -0.5, 0.75, (), jnp.float32),
        "attn_query": draw_attn_query(jax.random.fold_in(jax.random.fold_in(splits[11], part), 71), part),
        "attn_key": draw_attn_key(jax.random.fold_in(jax.random.fold_in(splits[11], part), 71), part),
        "attn_value": scatter_about(own_keys[8], (TOKENS, D), 1.0, 6.0, ((0, 16),)),
        "gain_ttt": jnp.clip(1.0 + 0.1 * jax.random.normal(splits[9], (D,), jnp.float32), 0.5, 1.5),
        "gain_attn": jnp.clip(1.0 + 0.1 * jax.random.normal(splits[10], (D,), jnp.float32), 0.5, 1.5),
    }


def ttt_step(weight, item):
    query, keys, values, rates = item
    high = lax.Precision.HIGHEST
    grads = jnp.einsum('shd,hde->she', keys, weight, precision=high) - values
    base = jnp.einsum('shd,hde->she', query, weight, precision=high)
    inner = jnp.einsum('thd,shd->hts', query, keys, precision=high) * jnp.transpose(rates)[:, None, :]
    lower = jnp.arange(query.shape[0])[:, None] >= jnp.arange(query.shape[0])[None, :]
    inner = jnp.where(lower[None], inner, 0.0)
    output = base - jnp.einsum('hts,she->the', inner, grads, precision=high)
    weight = weight - jnp.einsum('shd,she->hde', keys * rates[..., None], grads, precision=high)
    return (weight, output)

def window_attention(query, keys, values, valid_from):
    rows = query.shape[0]
    span = keys.shape[0]
    group = min(8, HEADS)
    q_three = query.reshape(rows, HEADS, HD)
    k_three = keys.reshape(span, HEADS, HD)
    v_three = values.reshape(span, HEADS, HD)
    offset = jnp.arange(rows, dtype=jnp.int32)[:, None] - jnp.arange(span, dtype=jnp.int32)[None, :] + (span - rows)
    column = jnp.arange(span, dtype=jnp.int32)[None, :]
    allowed = (offset >= 0) & (offset < span - rows) & (column >= valid_from)
    pieces = []
    for start in range(0, HEADS, group):
        q_group = q_three[:, start:start + group, :]
        k_group = k_three[:, start:start + group, :]
        v_group = v_three[:, start:start + group, :]
        scores = jnp.einsum('qhd,khd->hqk', q_group, k_group, preferred_element_type=jnp.float32) / math.sqrt(HD)
        scores = jnp.where(allowed[None], scores, -1e+30)
        largest = lax.optimization_barrier(jnp.max(scores, axis=-1, keepdims=True))
        expo = jnp.exp(scores - largest)
        totals = lax.optimization_barrier(jnp.sum(expo, axis=-1))
        weights = expo.astype(jnp.bfloat16)
        mixed = jnp.einsum('hqk,khd->qhd', weights, v_group, preferred_element_type=jnp.float32)
        pieces.append(mixed / jnp.transpose(totals)[:, :, None])
    return jnp.concatenate(pieces, axis=1)

def normed(values):
    return values * lax.rsqrt(lax.optimization_barrier(jnp.mean(values * values, axis=-1, keepdims=True)) + 1e-05)

def blend(ttt_out, attn_out, gain_ttt, gain_attn):
    rows = ttt_out.shape[0]
    first = normed(ttt_out).reshape(rows, HEADS * HD) * gain_ttt
    second = normed(attn_out).reshape(rows, HEADS * HD) * gain_attn
    return (0.5 * (first + second)).astype(jnp.bfloat16)

def prepare(ttt_query, ttt_key, ttt_value, lr_logit, lr_base):
    count = ttt_query.shape[0] // MB
    query = ttt_query.astype(jnp.float32).reshape(count, MB, HEADS, HD)
    keys = ttt_key.astype(jnp.float32).reshape(count, MB, HEADS, HD)
    keys = keys * lax.rsqrt(lax.optimization_barrier(jnp.mean(keys * keys, axis=-1, keepdims=True)) + 1e-06) / math.sqrt(HD)
    values = ttt_value.astype(jnp.float32).reshape(count, MB, HEADS, HD)
    rates = (lr_base[None, :] * jax.nn.sigmoid(lr_logit)).reshape(count, MB, HEADS)
    return (query, keys, values, rates)

def reference(ttt_query, ttt_key, ttt_value, lr_logit, lr_base, init_weight, attn_query, attn_key, attn_value, gain_ttt, gain_attn):
    query, keys, values, rates = prepare(ttt_query, ttt_key, ttt_value, lr_logit, lr_base)
    _, ttt_out = lax.scan(ttt_step, init_weight, (query, keys, values, rates))
    ttt_out = ttt_out.reshape(TOKENS, HEADS, HD)
    front = jnp.zeros((WIN_BLOCKS * L_DEV, D), jnp.bfloat16)
    padded_keys = jnp.concatenate([front, attn_key], axis=0)
    padded_values = jnp.concatenate([front, attn_value], axis=0)

    def one_block(block):
        begin = (block * L_DEV).astype(jnp.int32)
        q_block = lax.dynamic_slice_in_dim(attn_query, begin, L_DEV, 0)
        k_block = lax.dynamic_slice_in_dim(padded_keys, begin, (WIN_BLOCKS + 1) * L_DEV, 0)
        v_block = lax.dynamic_slice_in_dim(padded_values, begin, (WIN_BLOCKS + 1) * L_DEV, 0)
        valid_from = ((WIN_BLOCKS - block) * L_DEV).astype(jnp.int32)
        return window_attention(q_block, k_block, v_block, valid_from)
    attn_out = lax.map(one_block, jnp.arange(N_CTX, dtype=jnp.int32)).reshape(TOKENS, HEADS, HD)
    return blend(ttt_out, attn_out, gain_ttt, gain_attn)
```

```python
import functools
import math

import jax
import jax.numpy as jnp
from jax import lax
from jax.experimental import pallas as pl
from jax.experimental.pallas import tpu as pltpu
from jax.sharding import PartitionSpec as P

HD = 64
MB = 16
PAIR = 2 * HD
CHUNK = 2
F32 = jnp.float32
BF16 = jnp.bfloat16


def mm(a, b):
    return jnp.dot(a, b, preferred_element_type=F32)


def mmt(a, b):
    return lax.dot_general(a, b, (((1,), (1,)), ((), ())), preferred_element_type=F32)


def split(x):
    high = x.astype(BF16)
    return high, (x - high.astype(F32)).astype(BF16)


def stack_right(high, low):
    top = jnp.concatenate([high, low], axis=1)
    bottom = jnp.concatenate([high, jnp.zeros_like(low)], axis=1)
    return jnp.concatenate([top, bottom], axis=0)


def fold(x):
    half = x.shape[1] // 2
    return x[:, :half] + x[:, half:]


def dot_split(a, right):
    return fold(mm(jnp.concatenate(split(a), axis=1), right))


def dot_full(a, b):
    return dot_split(a, stack_right(*split(b)))


def swap(x):
    return pltpu.roll(x, HD, 1)


def kernel(
    count,
    tq_ref,
    tk_ref,
    tv_ref,
    logit_ref,
    base_ref,
    init_ref,
    aq_ref,
    ak_ref,
    av_ref,
    gt_ref,
    ga_ref,
    out_ref,
    kbuf,
    vbuf,
    eta_ref,
    z_ref,
    b_ref,
    p_ref,
    r_ref,
    att_ref,
    win,
    wout,
    kv_send,
    kv_recv,
    w_send,
    w_recv,
):
    rows, width = tq_ref.shape
    pairs = width // PAIR
    chunks = pairs // CHUNK
    heads = width // HD
    me = lax.axis_index("ctx")

    barrier = pltpu.get_barrier_semaphore()
    for back in (1, 2):

        @pl.when(me >= back)
        def _():
            pl.semaphore_signal(
                barrier,
                inc=1,
                device_id={"ctx": me - back},
                device_id_type=pl.DeviceIdType.MESH,
            )

    @pl.when(me + 1 < count)
    def _():
        pl.semaphore_wait(barrier, jnp.minimum(count - 1 - me, 2))

    def kv_copy(ahead, which):
        source, target = ((ak_ref, kbuf), (av_ref, vbuf))[which]
        at = 2 * (ahead - 1) + which
        return pltpu.make_async_remote_copy(
            src_ref=source,
            dst_ref=target.at[2 - ahead],
            send_sem=kv_send.at[at],
            recv_sem=kv_recv.at[at],
            device_id={"ctx": me + ahead},
            device_id_type=pl.DeviceIdType.MESH,
        )

    for ahead in (1, 2):

        @pl.when(me + ahead < count)
        def _():
            for which in range(2):
                kv_copy(ahead, which).start()

        @pl.when(me < ahead)
        def _():
            kbuf[2 - ahead] = jnp.zeros((rows, width), BF16)
            vbuf[2 - ahead] = jnp.zeros((rows, width), BF16)

    def w_copy(chunk):
        span = pl.ds(chunk * CHUNK, CHUNK)
        return pltpu.make_async_remote_copy(
            src_ref=wout.at[span],
            dst_ref=win.at[span],
            send_sem=w_send.at[chunk],
            recv_sem=w_recv.at[chunk],
            device_id={"ctx": me + 1},
            device_id_type=pl.DeviceIdType.MESH,
        )

    @pl.when(me == 0)
    def _():
        @pl.loop(0, pairs)
        def _(p):
            win[p] = jnp.concatenate([init_ref[2 * p], init_ref[2 * p + 1]], axis=1)

    eta_ref[...] = base_ref[...] * jax.nn.sigmoid(logit_ref[...])

    row = lax.broadcasted_iota(jnp.int32, (rows, rows), 0)
    col = lax.broadcasted_iota(jnp.int32, (rows, rows), 1)
    lane = lax.broadcasted_iota(jnp.int32, (rows, PAIR), 1)
    head_lane = lax.broadcasted_iota(jnp.int32, (rows, heads), 1)
    first = lane < HD
    first_w = first[:HD]
    lower = row >= col

    def columns(p):
        return pl.ds(pl.multiple_of(p * PAIR, PAIR), PAIR)

    def keep(half, x):
        return jnp.where(first, x, 0.0) if half == 0 else jnp.where(first, 0.0, x)

    def head_sum(half, x):
        return jnp.sum(keep(half, x), axis=1, keepdims=True)

    @pl.loop(0, pairs // 2)
    def _(step):
        items = []
        for u in range(2):
            p = step * 2 + u
            cols = columns(p)
            kp, qp = tk_ref[:, cols], tq_ref[:, cols]
            kf, qf = kp.astype(F32), qp.astype(F32)
            vf = tv_ref[:, cols].astype(F32)
            kt = jnp.transpose(kf).astype(BF16)
            square = kf * kf
            for half in range(2):
                scale = lax.rsqrt(head_sum(half, square) * (1.0 / HD) + 1e-6) * (1.0 / math.sqrt(HD))
                eta = jnp.sum(
                    jnp.where(head_lane == 2 * p + half, eta_ref[...], 0.0), axis=1, keepdims=True
                )
                own = keep(half, kf).astype(BF16)
                near = scale * eta
                rate = near * scale
                gram = jnp.where((row // MB) > (col // MB), mmt(own, kp) * rate, 0.0)
                cross = jnp.where(lower, mmt(qp, own), 0.0)
                k_low = kf if half == 0 else swap(kf)
                q_low = qf if half == 0 else swap(qf)
                v_high = swap(vf) if half == 0 else vf
                right = jnp.where(first, rate * k_low, near * v_high)
                items.append([gram, cross, right, kt, q_low])
        size = MB
        inverse = [jnp.where(row == col, 1.0, 0.0)] * len(items)
        while size < rows:
            band = ((row // (2 * size)) == (col // (2 * size))) & ((row // size) != (col // size))
            parts = [jnp.where(band, item[0], 0.0) for item in items]
            if size == MB:
                inverse = [a - part for a, part in zip(inverse, parts)]
            else:
                rights = [stack_right(*split(a)) for a in inverse]
                parts = [dot_full(a, part) for a, part in zip(inverse, parts)]
                parts = [dot_split(part, r) for part, r in zip(parts, rights)]
                inverse = [a - part for a, part in zip(inverse, parts)]
            size *= 2
        solved = [split(dot_full(a, item[2])) for a, item in zip(inverse, items)]
        moved = [fold(mm(item[3], jnp.concatenate(y, axis=1))) for item, y in zip(items, solved)]
        seen = [dot_split(item[1], stack_right(*y)) for item, y in zip(items, solved)]
        for u in range(2):
            p = step * 2 + u
            for half in range(2):
                rest = items[2 * u + half][4] - seen[2 * u + half]
                high = rest.astype(BF16).astype(F32)
                p_ref[p, half * rows : (half + 1) * rows] = jnp.where(
                    first, high, swap(rest - high)
                ).astype(BF16)
            r_ref[:, columns(p)] = jnp.where(first, swap(seen[2 * u]), seen[2 * u + 1])
            z_one, z_two = moved[2 * u][:HD], moved[2 * u + 1][HD:]
            b_ref[p] = jnp.where(first_w, swap(z_one), z_two)
            z = jnp.concatenate([z_one, z_two], axis=0)
            high = z.astype(BF16).astype(F32)
            z_ref[p] = jnp.where(
                lax.broadcasted_iota(jnp.int32, z.shape, 1) < HD, high, swap(z - high)
            ).astype(BF16)

    for ahead in (1, 2):

        @pl.when(me >= ahead)
        def _():
            for which in range(2):
                kv_copy(ahead, which).wait_recv()

    has_far = me >= 2
    has_near = me >= 1

    def attend(p, carry):
        cols = columns(p)
        qf = aq_ref[:, cols].astype(F32) * (1.0 / math.sqrt(HD))
        k_far, k_near, k_own = kbuf[0, :, cols], kbuf[1, :, cols], ak_ref[:, cols]
        v_ends = jnp.concatenate([av_ref[:, cols], vbuf[0, :, cols]], axis=0)
        v_near = vbuf[1, :, cols]
        outs = []
        for half in range(2):
            q = keep(half, qf).astype(BF16)
            far = jnp.where(has_far, mmt(q, k_far), -1e30)
            near = jnp.where(has_near, mmt(q, k_near), -1e30)
            ends = jnp.where(lower, mmt(q, k_own), far)
            largest = jnp.max(jnp.maximum(ends, near), axis=1, keepdims=True)
            e_ends = jnp.exp(ends - largest)
            e_near = jnp.exp(near - largest)
            total = jnp.sum(e_ends + e_near, axis=1, keepdims=True)
            weights = jnp.concatenate(
                [jnp.where(lower, e_ends, 0.0).astype(BF16), jnp.where(lower, 0.0, e_ends).astype(BF16)],
                axis=1,
            )
            outs.append((mm(weights, v_ends) + mm(e_near.astype(BF16), v_near)) / total)
        x = jnp.where(first, outs[0], outs[1])
        att_ref[:, cols] = normed(x) * (ga_ref[:, cols] * 0.5)
        return carry

    def normed(x):
        square = x * x
        mean = jnp.where(first, head_sum(0, square), head_sum(1, square)) * (1.0 / HD)
        return x * lax.rsqrt(mean + 1e-5)

    early = jnp.minimum(jnp.maximum(2 * (me - 6), 0), pairs)
    lax.fori_loop(0, early, attend, 0)

    @pl.loop(0, chunks)
    def _(chunk):
        @pl.when(me > 0)
        def _():
            w_copy(chunk).wait_recv()

        @pl.when(me + 1 < count)
        def _():
            for u in range(CHUNK):
                p = chunk * CHUNK + u
                w = win[p]
                r = fold(mm(z_ref[p], stack_right(*split(w))))
                wout[p] = w - jnp.where(first_w, r[:HD], r[HD:]) + b_ref[p]
            w_copy(chunk).start()

    lax.fori_loop(early, pairs, attend, 0)

    def finish(p, carry):
        cols = columns(p)
        r = fold(mm(p_ref[p], stack_right(*split(win[p]))))
        x = jnp.where(first, r[:rows], r[rows:]) + r_ref[:, cols]
        out_ref[:, cols] = (normed(x) * (gt_ref[:, cols] * 0.5) + att_ref[:, cols]).astype(BF16)
        return carry

    lax.fori_loop(0, pairs, finish, 0)

    @pl.when(me + 1 < count)
    def _():
        @pl.loop(0, chunks)
        def _(chunk):
            w_copy(chunk).wait_send()

    for ahead in (1, 2):

        @pl.when(me + ahead < count)
        def _():
            for which in range(2):
                kv_copy(ahead, which).wait_send()


def per_device(*args):
    (tq, tk, tv, logit, base, init, aq, ak, av, gain_ttt, gain_attn) = args
    rows, width = tq.shape
    pairs = width // PAIR
    chunks = pairs // CHUNK
    count = lax.axis_size("ctx")
    vmem = pl.BlockSpec(memory_space=pltpu.VMEM)
    return pl.pallas_call(
        functools.partial(kernel, count),
        out_shape=jax.ShapeDtypeStruct((rows, width), BF16),
        in_specs=[vmem] * 11,
        out_specs=vmem,
        scratch_shapes=[
            pltpu.VMEM((2, rows, width), BF16),
            pltpu.VMEM((2, rows, width), BF16),
            pltpu.VMEM(logit.shape, F32),
            pltpu.VMEM((pairs, PAIR, PAIR), BF16),
            pltpu.VMEM((pairs, HD, PAIR), F32),
            pltpu.VMEM((pairs, 2 * rows, PAIR), BF16),
            pltpu.VMEM((rows, width), F32),
            pltpu.VMEM((rows, width), F32),
            pltpu.VMEM((pairs, HD, PAIR), F32),
            pltpu.VMEM((pairs, HD, PAIR), F32),
            pltpu.SemaphoreType.DMA((4,)),
            pltpu.SemaphoreType.DMA((4,)),
            pltpu.SemaphoreType.DMA((chunks,)),
            pltpu.SemaphoreType.DMA((chunks,)),
        ],
        compiler_params=pltpu.CompilerParams(
            collective_id=0, has_side_effects=True, vmem_limit_bytes=48 * 1024 * 1024
        ),
    )(tq, tk, tv, logit, base[None], init, aq, ak, av, gain_ttt[None], gain_attn[None])


def solution(mesh):
    split_rows = P(("groups", "ctx"), None)
    in_specs = (split_rows,) * 4 + (P(), P()) + (split_rows,) * 3 + (P(), P())
    return jax.shard_map(
        per_device, mesh=mesh, in_specs=in_specs, out_specs=split_rows, check_vma=False
    )
```

```python
import functools
import math

import jax
import jax.numpy as jnp
from jax import lax
from jax.experimental import pallas as pl
from jax.experimental.pallas import tpu as pltpu
from jax.sharding import PartitionSpec as P

HD = 64
MB = 16
PAIR = 2 * HD
CHUNK = 2
F32 = jnp.float32
BF16 = jnp.bfloat16


def mm(a, b):
    return jnp.dot(a, b, preferred_element_type=F32)


def mmt(a, b):
    return lax.dot_general(a, b, (((1,), (1,)), ((), ())), preferred_element_type=F32)


def split(x):
    high = x.astype(BF16)
    return high, (x - high.astype(F32)).astype(BF16)


def stack_right(high, low):
    top = jnp.concatenate([high, low], axis=1)
    bottom = jnp.concatenate([high, jnp.zeros_like(low)], axis=1)
    return jnp.concatenate([top, bottom], axis=0)


def fold(x):
    half = x.shape[1] // 2
    return x[:, :half] + x[:, half:]


def dot_split(a, right):
    return fold(mm(jnp.concatenate(split(a), axis=1), right))


def dot_full(a, b):
    return dot_split(a, stack_right(*split(b)))


def swap(x):
    return pltpu.roll(x, HD, 1)


def kernel(
    count,
    tq_ref,
    tk_ref,
    tv_ref,
    logit_ref,
    base_ref,
    init_ref,
    aq_hbm,
    ak_hbm,
    av_hbm,
    gt_ref,
    ga_ref,
    out_ref,
    aq_ref,
    ak_ref,
    av_ref,
    kbuf,
    vbuf,
    eta_ref,
    z_ref,
    b_ref,
    p_ref,
    r_ref,
    att_ref,
    win,
    wout,
    kv_send,
    kv_recv,
    w_send,
    w_recv,
    own_sem,
):
    rows, width = tq_ref.shape
    pairs = width // PAIR
    chunks = pairs // CHUNK
    heads = width // HD
    me = lax.axis_index("ctx")

    even = lax.rem(me, 2) == 0
    odd = jnp.logical_not(even)
    has_far = me >= 2
    has_near = me >= 1
    sends_far = me + 2 < count
    mirrors = jnp.logical_and(odd, has_far)

    own_copies = [
        pltpu.make_async_copy(source, target, own_sem.at[at])
        for at, (source, target) in enumerate(
            ((aq_hbm, aq_ref), (ak_hbm, ak_ref), (av_hbm, av_ref))
        )
    ]
    for copy in own_copies:
        copy.start()

    barrier = pltpu.get_barrier_semaphore()

    def greet(offset):
        pl.semaphore_signal(
            barrier, inc=1, device_id={"ctx": me + offset}, device_id_type=pl.DeviceIdType.MESH
        )

    pl.when(has_near)(lambda: greet(-1))
    pl.when(has_far)(lambda: greet(-2))
    pl.when(jnp.logical_and(even, has_far))(lambda: greet(1))
    peers = (
        (me + 1 < count).astype(jnp.int32) + sends_far.astype(jnp.int32) + mirrors.astype(jnp.int32)
    )

    @pl.when(peers > 0)
    def _():
        pl.semaphore_wait(barrier, peers)

    def kv_copy(slot, which, source, target):
        at = 2 * slot + which
        return pltpu.make_async_remote_copy(
            src_ref=source,
            dst_ref=(kbuf, vbuf)[which].at[slot],
            send_sem=kv_send.at[at],
            recv_sem=kv_recv.at[at],
            device_id={"ctx": target},
            device_id_type=pl.DeviceIdType.MESH,
        )

    def far_copy(which):
        return kv_copy(0, which, (ak_hbm, av_hbm)[which], me + 2)

    def near_copy(which):
        return kv_copy(1, which, (ak_hbm, av_hbm)[which], me + 1)

    def mirror_copy(which):
        return kv_copy(1, which, (kbuf, vbuf)[which].at[0], me - 1)

    @pl.when(sends_far)
    def _():
        for which in range(2):
            far_copy(which).start()

    @pl.when(even)
    def _():
        for which in range(2):
            near_copy(which).start()

    for slot, ready in ((0, has_far), (1, has_near)):

        @pl.when(jnp.logical_not(ready))
        def _():
            kbuf[slot] = jnp.zeros((rows, width), BF16)
            vbuf[slot] = jnp.zeros((rows, width), BF16)

    def w_copy(chunk):
        span = pl.ds(chunk * CHUNK, CHUNK)
        return pltpu.make_async_remote_copy(
            src_ref=wout.at[span],
            dst_ref=win.at[span],
            send_sem=w_send.at[chunk],
            recv_sem=w_recv.at[chunk],
            device_id={"ctx": me + 1},
            device_id_type=pl.DeviceIdType.MESH,
        )

    @pl.when(me == 0)
    def _():
        @pl.loop(0, pairs)
        def _(p):
            win[p] = jnp.concatenate([init_ref[2 * p], init_ref[2 * p + 1]], axis=1)

    eta_ref[...] = base_ref[...] * jax.nn.sigmoid(logit_ref[...])

    row = lax.broadcasted_iota(jnp.int32, (rows, rows), 0)
    col = lax.broadcasted_iota(jnp.int32, (rows, rows), 1)
    lane = lax.broadcasted_iota(jnp.int32, (rows, PAIR), 1)
    head_lane = lax.broadcasted_iota(jnp.int32, (rows, heads), 1)
    first = lane < HD
    first_w = first[:HD]
    lower = row >= col

    def columns(p):
        return pl.ds(pl.multiple_of(p * PAIR, PAIR), PAIR)

    def keep(half, x):
        return jnp.where(first, x, 0.0) if half == 0 else jnp.where(first, 0.0, x)

    def head_sum(half, x):
        return jnp.sum(keep(half, x), axis=1, keepdims=True)

    @pl.loop(0, pairs // 2)
    def _(step):
        items = []
        for u in range(2):
            p = step * 2 + u
            cols = columns(p)
            kp, qp = tk_ref[:, cols], tq_ref[:, cols]
            kf, qf = kp.astype(F32), qp.astype(F32)
            vf = tv_ref[:, cols].astype(F32)
            kt = jnp.transpose(kf).astype(BF16)
            square = kf * kf
            for half in range(2):
                scale = lax.rsqrt(head_sum(half, square) * (1.0 / HD) + 1e-6) * (1.0 / math.sqrt(HD))
                eta = jnp.sum(
                    jnp.where(head_lane == 2 * p + half, eta_ref[...], 0.0), axis=1, keepdims=True
                )
                own = keep(half, kf).astype(BF16)
                near = scale * eta
                rate = near * scale
                gram = jnp.where((row // MB) > (col // MB), mmt(own, kp) * rate, 0.0)
                cross = jnp.where(lower, mmt(qp, own), 0.0)
                k_low = kf if half == 0 else swap(kf)
                q_low = qf if half == 0 else swap(qf)
                v_high = swap(vf) if half == 0 else vf
                right = jnp.where(first, rate * k_low, near * v_high)
                items.append([gram, cross, right, kt, q_low])
        size = MB
        inverse = [jnp.where(row == col, 1.0, 0.0)] * len(items)
        while size < rows:
            band = ((row // (2 * size)) == (col // (2 * size))) & ((row // size) != (col // size))
            parts = [jnp.where(band, item[0], 0.0) for item in items]
            if size == MB:
                inverse = [a - part for a, part in zip(inverse, parts)]
            else:
                rights = [stack_right(*split(a)) for a in inverse]
                parts = [dot_full(a, part) for a, part in zip(inverse, parts)]
                parts = [dot_split(part, r) for part, r in zip(parts, rights)]
                inverse = [a - part for a, part in zip(inverse, parts)]
            size *= 2
        solved = [split(dot_full(a, item[2])) for a, item in zip(inverse, items)]
        moved = [fold(mm(item[3], jnp.concatenate(y, axis=1))) for item, y in zip(items, solved)]
        seen = [dot_split(item[1], stack_right(*y)) for item, y in zip(items, solved)]
        for u in range(2):
            p = step * 2 + u
            for half in range(2):
                rest = items[2 * u + half][4] - seen[2 * u + half]
                high = rest.astype(BF16).astype(F32)
                p_ref[p, half * rows : (half + 1) * rows] = jnp.where(
                    first, high, swap(rest - high)
                ).astype(BF16)
            r_ref[:, columns(p)] = jnp.where(first, swap(seen[2 * u]), seen[2 * u + 1])
            z_one, z_two = moved[2 * u][:HD], moved[2 * u + 1][HD:]
            b_ref[p] = jnp.where(first_w, swap(z_one), z_two)
            z = jnp.concatenate([z_one, z_two], axis=0)
            high = z.astype(BF16).astype(F32)
            z_ref[p] = jnp.where(
                lax.broadcasted_iota(jnp.int32, z.shape, 1) < HD, high, swap(z - high)
            ).astype(BF16)

    def take_window():
        @pl.when(has_far)
        def _():
            for which in range(2):
                far_copy(which).wait_recv()

        @pl.when(mirrors)
        def _():
            for which in range(2):
                mirror_copy(which).start()

        @pl.when(has_near)
        def _():
            for which in range(2):
                near_copy(which).wait_recv()

    for copy in own_copies:
        copy.wait()

    def attend(p, carry):
        cols = columns(p)
        qf = aq_ref[:, cols].astype(F32) * (1.0 / math.sqrt(HD))
        k_far, k_near, k_own = kbuf[0, :, cols], kbuf[1, :, cols], ak_ref[:, cols]
        v_ends = jnp.concatenate([av_ref[:, cols], vbuf[0, :, cols]], axis=0)
        v_near = vbuf[1, :, cols]
        outs = []
        for half in range(2):
            q = keep(half, qf).astype(BF16)
            far = jnp.where(has_far, mmt(q, k_far), -1e30)
            near = jnp.where(has_near, mmt(q, k_near), -1e30)
            ends = jnp.where(lower, mmt(q, k_own), far)
            largest = jnp.max(jnp.maximum(ends, near), axis=1, keepdims=True)
            e_ends = jnp.exp(ends - largest)
            e_near = jnp.exp(near - largest)
            total = jnp.sum(e_ends + e_near, axis=1, keepdims=True)
            weights = jnp.concatenate(
                [jnp.where(lower, e_ends, 0.0).astype(BF16), jnp.where(lower, 0.0, e_ends).astype(BF16)],
                axis=1,
            )
            outs.append((mm(weights, v_ends) + mm(e_near.astype(BF16), v_near)) / total)
        x = jnp.where(first, outs[0], outs[1])
        att_ref[:, cols] = normed(x) * (ga_ref[:, cols] * 0.5)
        return carry

    def normed(x):
        square = x * x
        mean = jnp.where(first, head_sum(0, square), head_sum(1, square)) * (1.0 / HD)
        return x * lax.rsqrt(mean + 1e-5)

    window_first = me >= 11
    early = jnp.where(window_first, jnp.minimum(2 * (me - 11), pairs // 2), 0)
    pl.when(window_first)(take_window)
    lax.fori_loop(0, early, attend, 0)

    @pl.loop(0, chunks)
    def _(chunk):
        @pl.when(me > 0)
        def _():
            w_copy(chunk).wait_recv()

        @pl.when(me + 1 < count)
        def _():
            for u in range(CHUNK):
                p = chunk * CHUNK + u
                w = win[p]
                r = fold(mm(z_ref[p], stack_right(*split(w))))
                wout[p] = w - jnp.where(first_w, r[:HD], r[HD:]) + b_ref[p]
            w_copy(chunk).start()

    pl.when(jnp.logical_not(window_first))(take_window)
    lax.fori_loop(early, pairs, attend, 0)

    def finish(p, carry):
        cols = columns(p)
        r = fold(mm(p_ref[p], stack_right(*split(win[p]))))
        x = jnp.where(first, r[:rows], r[rows:]) + r_ref[:, cols]
        out_ref[:, cols] = (normed(x) * (gt_ref[:, cols] * 0.5) + att_ref[:, cols]).astype(BF16)
        return carry

    lax.fori_loop(0, pairs, finish, 0)

    @pl.when(me + 1 < count)
    def _():
        @pl.loop(0, chunks)
        def _(chunk):
            w_copy(chunk).wait_send()

    @pl.when(sends_far)
    def _():
        for which in range(2):
            far_copy(which).wait_send()

    @pl.when(even)
    def _():
        for which in range(2):
            near_copy(which).wait_send()

    @pl.when(mirrors)
    def _():
        for which in range(2):
            mirror_copy(which).wait_send()


def per_device(*args):
    (tq, tk, tv, logit, base, init, aq, ak, av, gain_ttt, gain_attn) = args
    rows, width = tq.shape
    pairs = width // PAIR
    chunks = pairs // CHUNK
    count = lax.axis_size("ctx")
    vmem = pl.BlockSpec(memory_space=pltpu.VMEM)
    hbm = pl.BlockSpec(memory_space=pltpu.HBM)
    return pl.pallas_call(
        functools.partial(kernel, count),
        out_shape=jax.ShapeDtypeStruct((rows, width), BF16),
        in_specs=[vmem] * 6 + [hbm] * 3 + [vmem] * 2,
        out_specs=vmem,
        scratch_shapes=[
            pltpu.VMEM((rows, width), BF16),
            pltpu.VMEM((rows, width), BF16),
            pltpu.VMEM((rows, width), BF16),
            pltpu.VMEM((2, rows, width), BF16),
            pltpu.VMEM((2, rows, width), BF16),
            pltpu.VMEM(logit.shape, F32),
            pltpu.VMEM((pairs, PAIR, PAIR), BF16),
            pltpu.VMEM((pairs, HD, PAIR), F32),
            pltpu.VMEM((pairs, 2 * rows, PAIR), BF16),
            pltpu.VMEM((rows, width), F32),
            pltpu.VMEM((rows, width), F32),
            pltpu.VMEM((pairs, HD, PAIR), F32),
            pltpu.VMEM((pairs, HD, PAIR), F32),
            pltpu.SemaphoreType.DMA((4,)),
            pltpu.SemaphoreType.DMA((4,)),
            pltpu.SemaphoreType.DMA((chunks,)),
            pltpu.SemaphoreType.DMA((chunks,)),
            pltpu.SemaphoreType.DMA((3,)),
        ],
        compiler_params=pltpu.CompilerParams(
            collective_id=0, has_side_effects=True, vmem_limit_bytes=48 * 1024 * 1024
        ),
    )(tq, tk, tv, logit, base[None], init, aq, ak, av, gain_ttt[None], gain_attn[None])


def solution(mesh):
    split_rows = P(("groups", "ctx"), None)
    in_specs = (split_rows,) * 4 + (P(), P()) + (split_rows,) * 3 + (P(), P())
    return jax.shard_map(
        per_device, mesh=mesh, in_specs=in_specs, out_specs=split_rows, check_vma=False
    )
```

```python
import functools
import math

import jax
import jax.numpy as jnp
from jax import lax
from jax.experimental import pallas as pl
from jax.experimental.pallas import tpu as pltpu
from jax.sharding import PartitionSpec as P

HD = 64
MB = 16
PAIR = 2 * HD
CHUNK = 2
F32 = jnp.float32
BF16 = jnp.bfloat16


def mm(a, b):
    return jnp.dot(a, b, preferred_element_type=F32)


def mmt(a, b):
    return lax.dot_general(a, b, (((1,), (1,)), ((), ())), preferred_element_type=F32)


def split(x):
    high = x.astype(BF16)
    return high, (x - high.astype(F32)).astype(BF16)


def stack_right(high, low):
    top = jnp.concatenate([high, low], axis=1)
    bottom = jnp.concatenate([high, jnp.zeros_like(low)], axis=1)
    return jnp.concatenate([top, bottom], axis=0)


def fold(x):
    half = x.shape[1] // 2
    return x[:, :half] + x[:, half:]


def dot_split(a, right):
    return fold(mm(jnp.concatenate(split(a), axis=1), right))


def dot_full(a, b):
    return dot_split(a, stack_right(*split(b)))


def swap(x):
    return pltpu.roll(x, HD, 1)


def kernel(
    count,
    tq_ref,
    tk_ref,
    tv_ref,
    logit_ref,
    base_ref,
    init_ref,
    aq_hbm,
    ak_hbm,
    av_hbm,
    gt_ref,
    ga_ref,
    out_ref,
    aq_ref,
    ak_ref,
    av_ref,
    kbuf,
    vbuf,
    eta_ref,
    z_ref,
    b_ref,
    p_ref,
    r_ref,
    att_ref,
    win,
    wout,
    kv_send,
    kv_recv,
    w_send,
    w_recv,
    own_sem,
):
    rows, width = tq_ref.shape
    pairs = width // PAIR
    chunks = pairs // CHUNK
    heads = width // HD
    me = lax.axis_index("ctx")

    even = lax.rem(me, 2) == 0
    odd = jnp.logical_not(even)
    has_far = me >= 2
    has_near = me >= 1
    sends_far = me + 2 < count
    mirrors = jnp.logical_and(odd, has_far)

    own_copies = [
        pltpu.make_async_copy(source, target, own_sem.at[at])
        for at, (source, target) in enumerate(
            ((aq_hbm, aq_ref), (ak_hbm, ak_ref), (av_hbm, av_ref))
        )
    ]
    for copy in own_copies:
        copy.start()

    barrier = pltpu.get_barrier_semaphore()

    def greet(offset):
        pl.semaphore_signal(
            barrier, inc=1, device_id={"ctx": me + offset}, device_id_type=pl.DeviceIdType.MESH
        )

    pl.when(has_near)(lambda: greet(-1))
    pl.when(has_far)(lambda: greet(-2))
    pl.when(jnp.logical_and(even, has_far))(lambda: greet(1))
    peers = (
        (me + 1 < count).astype(jnp.int32) + sends_far.astype(jnp.int32) + mirrors.astype(jnp.int32)
    )

    @pl.when(peers > 0)
    def _():
        pl.semaphore_wait(barrier, peers)

    def kv_copy(slot, item, source, target):
        which, part = item % 2, item // 2
        at = 4 * slot + item
        span = pl.ds(part * (width // 2), width // 2)
        return pltpu.make_async_remote_copy(
            src_ref=source.at[:, span],
            dst_ref=(kbuf, vbuf)[which].at[slot, :, span],
            send_sem=kv_send.at[at],
            recv_sem=kv_recv.at[at],
            device_id={"ctx": target},
            device_id_type=pl.DeviceIdType.MESH,
        )

    def far_copy(item):
        return kv_copy(0, item, (ak_hbm, av_hbm)[item % 2], me + 2)

    def near_copy(item):
        return kv_copy(1, item, (ak_hbm, av_hbm)[item % 2], me + 1)

    def mirror_copy(item):
        return kv_copy(1, item, (kbuf, vbuf)[item % 2].at[0], me - 1)

    @pl.when(sends_far)
    def _():
        for which in range(4):
            far_copy(which).start()

    @pl.when(even)
    def _():
        for which in range(4):
            near_copy(which).start()

    for slot, ready in ((0, has_far), (1, has_near)):

        @pl.when(jnp.logical_not(ready))
        def _():
            kbuf[slot] = jnp.zeros((rows, width), BF16)
            vbuf[slot] = jnp.zeros((rows, width), BF16)

    def w_copy(chunk):
        span = pl.ds(chunk * CHUNK, CHUNK)
        return pltpu.make_async_remote_copy(
            src_ref=wout.at[span],
            dst_ref=win.at[span],
            send_sem=w_send.at[chunk],
            recv_sem=w_recv.at[chunk],
            device_id={"ctx": me + 1},
            device_id_type=pl.DeviceIdType.MESH,
        )

    @pl.when(me == 0)
    def _():
        @pl.loop(0, pairs)
        def _(p):
            win[p] = jnp.concatenate([init_ref[2 * p], init_ref[2 * p + 1]], axis=1)

    eta_ref[...] = base_ref[...] * jax.nn.sigmoid(logit_ref[...])

    row = lax.broadcasted_iota(jnp.int32, (rows, rows), 0)
    col = lax.broadcasted_iota(jnp.int32, (rows, rows), 1)
    lane = lax.broadcasted_iota(jnp.int32, (rows, PAIR), 1)
    head_lane = lax.broadcasted_iota(jnp.int32, (rows, heads), 1)
    first = lane < HD
    first_w = first[:HD]
    lower = row >= col

    def columns(p):
        return pl.ds(pl.multiple_of(p * PAIR, PAIR), PAIR)

    def keep(half, x):
        return jnp.where(first, x, 0.0) if half == 0 else jnp.where(first, 0.0, x)

    def head_sum(half, x):
        return jnp.sum(keep(half, x), axis=1, keepdims=True)

    @pl.loop(0, pairs // 2)
    def _(step):
        items = []
        for u in range(2):
            p = step * 2 + u
            cols = columns(p)
            kp, qp = tk_ref[:, cols], tq_ref[:, cols]
            kf, qf = kp.astype(F32), qp.astype(F32)
            vf = tv_ref[:, cols].astype(F32)
            kt = jnp.transpose(kf).astype(BF16)
            square = kf * kf
            for half in range(2):
                scale = lax.rsqrt(head_sum(half, square) * (1.0 / HD) + 1e-6) * (1.0 / math.sqrt(HD))
                eta = jnp.sum(
                    jnp.where(head_lane == 2 * p + half, eta_ref[...], 0.0), axis=1, keepdims=True
                )
                own = keep(half, kf).astype(BF16)
                near = scale * eta
                rate = near * scale
                gram = jnp.where((row // MB) > (col // MB), mmt(own, kp) * rate, 0.0)
                cross = jnp.where(lower, mmt(qp, own), 0.0)
                k_low = kf if half == 0 else swap(kf)
                q_low = qf if half == 0 else swap(qf)
                v_high = swap(vf) if half == 0 else vf
                right = jnp.where(first, rate * k_low, near * v_high)
                items.append([gram, cross, right, kt, q_low])
        size = MB
        inverse = [jnp.where(row == col, 1.0, 0.0)] * len(items)
        while size < rows:
            band = ((row // (2 * size)) == (col // (2 * size))) & ((row // size) != (col // size))
            parts = [jnp.where(band, item[0], 0.0) for item in items]
            if size == MB:
                inverse = [a - part for a, part in zip(inverse, parts)]
            else:
                rights = [stack_right(*split(a)) for a in inverse]
                parts = [dot_full(a, part) for a, part in zip(inverse, parts)]
                parts = [dot_split(part, r) for part, r in zip(parts, rights)]
                inverse = [a - part for a, part in zip(inverse, parts)]
            size *= 2
        solved = [split(dot_full(a, item[2])) for a, item in zip(inverse, items)]
        moved = [fold(mm(item[3], jnp.concatenate(y, axis=1))) for item, y in zip(items, solved)]
        seen = [dot_split(item[1], stack_right(*y)) for item, y in zip(items, solved)]
        for u in range(2):
            p = step * 2 + u
            for half in range(2):
                rest = items[2 * u + half][4] - seen[2 * u + half]
                high = rest.astype(BF16).astype(F32)
                p_ref[p, half * rows : (half + 1) * rows] = jnp.where(
                    first, high, swap(rest - high)
                ).astype(BF16)
            r_ref[:, columns(p)] = jnp.where(first, swap(seen[2 * u]), seen[2 * u + 1])
            z_one, z_two = moved[2 * u][:HD], moved[2 * u + 1][HD:]
            b_ref[p] = jnp.where(first_w, swap(z_one), z_two)
            z = jnp.concatenate([z_one, z_two], axis=0)
            high = z.astype(BF16).astype(F32)
            z_ref[p] = jnp.where(
                lax.broadcasted_iota(jnp.int32, z.shape, 1) < HD, high, swap(z - high)
            ).astype(BF16)

    def take_window(part):
        @pl.when(has_far)
        def _():
            for which in (2 * part, 2 * part + 1):
                far_copy(which).wait_recv()

        @pl.when(mirrors)
        def _():
            for which in (2 * part, 2 * part + 1):
                mirror_copy(which).start()

        @pl.when(has_near)
        def _():
            for which in (2 * part, 2 * part + 1):
                near_copy(which).wait_recv()

    for copy in own_copies:
        copy.wait()

    def attend(p, carry):
        cols = columns(p)
        qf = aq_ref[:, cols].astype(F32) * (1.0 / math.sqrt(HD))
        k_far, k_near, k_own = kbuf[0, :, cols], kbuf[1, :, cols], ak_ref[:, cols]
        v_ends = jnp.concatenate([av_ref[:, cols], vbuf[0, :, cols]], axis=0)
        v_near = vbuf[1, :, cols]
        outs = []
        for half in range(2):
            q = keep(half, qf).astype(BF16)
            far = jnp.where(has_far, mmt(q, k_far), -1e30)
            near = jnp.where(has_near, mmt(q, k_near), -1e30)
            ends = jnp.where(lower, mmt(q, k_own), far)
            largest = jnp.max(jnp.maximum(ends, near), axis=1, keepdims=True)
            e_ends = jnp.exp(ends - largest)
            e_near = jnp.exp(near - largest)
            total = jnp.sum(e_ends + e_near, axis=1, keepdims=True)
            weights = jnp.concatenate(
                [jnp.where(lower, e_ends, 0.0).astype(BF16), jnp.where(lower, 0.0, e_ends).astype(BF16)],
                axis=1,
            )
            outs.append((mm(weights, v_ends) + mm(e_near.astype(BF16), v_near)) / total)
        x = jnp.where(first, outs[0], outs[1])
        att_ref[:, cols] = normed(x) * (ga_ref[:, cols] * 0.5)
        return carry

    def normed(x):
        square = x * x
        mean = jnp.where(first, head_sum(0, square), head_sum(1, square)) * (1.0 / HD)
        return x * lax.rsqrt(mean + 1e-5)

    window_first = me >= 11
    early = jnp.where(window_first, jnp.minimum(2 * (me - 11), pairs // 2), 0)
    pl.when(window_first)(lambda: take_window(0))
    lax.fori_loop(0, early, attend, 0)

    @pl.loop(0, chunks)
    def _(chunk):
        @pl.when(me > 0)
        def _():
            w_copy(chunk).wait_recv()

        @pl.when(me + 1 < count)
        def _():
            for u in range(CHUNK):
                p = chunk * CHUNK + u
                w = win[p]
                r = fold(mm(z_ref[p], stack_right(*split(w))))
                wout[p] = w - jnp.where(first_w, r[:HD], r[HD:]) + b_ref[p]
            w_copy(chunk).start()

    pl.when(jnp.logical_not(window_first))(lambda: take_window(0))
    lax.fori_loop(early, pairs // 2, attend, 0)
    take_window(1)
    lax.fori_loop(pairs // 2, pairs, attend, 0)

    def finish(p, carry):
        cols = columns(p)
        r = fold(mm(p_ref[p], stack_right(*split(win[p]))))
        x = jnp.where(first, r[:rows], r[rows:]) + r_ref[:, cols]
        out_ref[:, cols] = (normed(x) * (gt_ref[:, cols] * 0.5) + att_ref[:, cols]).astype(BF16)
        return carry

    lax.fori_loop(0, pairs, finish, 0)

    @pl.when(me + 1 < count)
    def _():
        @pl.loop(0, chunks)
        def _(chunk):
            w_copy(chunk).wait_send()

    @pl.when(sends_far)
    def _():
        for which in range(4):
            far_copy(which).wait_send()

    @pl.when(even)
    def _():
        for which in range(4):
            near_copy(which).wait_send()

    @pl.when(mirrors)
    def _():
        for which in range(4):
            mirror_copy(which).wait_send()


def per_device(*args):
    (tq, tk, tv, logit, base, init, aq, ak, av, gain_ttt, gain_attn) = args
    rows, width = tq.shape
    pairs = width // PAIR
    chunks = pairs // CHUNK
    count = lax.axis_size("ctx")
    vmem = pl.BlockSpec(memory_space=pltpu.VMEM)
    hbm = pl.BlockSpec(memory_space=pltpu.HBM)
    return pl.pallas_call(
        functools.partial(kernel, count),
        out_shape=jax.ShapeDtypeStruct((rows, width), BF16),
        in_specs=[vmem] * 6 + [hbm] * 3 + [vmem] * 2,
        out_specs=vmem,
        scratch_shapes=[
            pltpu.VMEM((rows, width), BF16),
            pltpu.VMEM((rows, width), BF16),
            pltpu.VMEM((rows, width), BF16),
            pltpu.VMEM((2, rows, width), BF16),
            pltpu.VMEM((2, rows, width), BF16),
            pltpu.VMEM(logit.shape, F32),
            pltpu.VMEM((pairs, PAIR, PAIR), BF16),
            pltpu.VMEM((pairs, HD, PAIR), F32),
            pltpu.VMEM((pairs, 2 * rows, PAIR), BF16),
            pltpu.VMEM((rows, width), F32),
            pltpu.VMEM((rows, width), F32),
            pltpu.VMEM((pairs, HD, PAIR), F32),
            pltpu.VMEM((pairs, HD, PAIR), F32),
            pltpu.SemaphoreType.DMA((8,)),
            pltpu.SemaphoreType.DMA((8,)),
            pltpu.SemaphoreType.DMA((chunks,)),
            pltpu.SemaphoreType.DMA((chunks,)),
            pltpu.SemaphoreType.DMA((3,)),
        ],
        compiler_params=pltpu.CompilerParams(
            collective_id=0, has_side_effects=True, vmem_limit_bytes=48 * 1024 * 1024
        ),
    )(tq, tk, tv, logit, base[None], init, aq, ak, av, gain_ttt[None], gain_attn[None])


def solution(mesh):
    split_rows = P(("groups", "ctx"), None)
    in_specs = (split_rows,) * 4 + (P(), P()) + (split_rows,) * 3 + (P(), P())
    return jax.shard_map(
        per_device, mesh=mesh, in_specs=in_specs, out_specs=split_rows, check_vma=False
    )
```
